32 devices in a mesh: dp: 4 (over z), expert: 8 (over y, x, core).
Axes of the slice: x: 2, y: 2, z: 4, core: 2. Of those that a mesh axis runs over, the one named last changes fastest.
Arguments:
- tokens: bfloat16 [128, 7168], P(('dp', 'expert')), may hold values from -6 to 6
- routes: int32 [128, 2], P(('dp', 'expert')), may hold values from 0 to 7, all different within a row; in each aligned block of 4 rows (0 to 3, 4 to 7, ...) at most 2 rows name the same one
- gate_scores: float32 [128, 2], P(('dp', 'expert')), may hold values from 0.1 to 1
- w_gate: bfloat16 [8, 7168, 2048], P('expert', None, 'dp'), may hold values from -0.0625 to 0.0625
- w_up: bfloat16 [8, 7168, 2048], P('expert', None, 'dp'), may hold values from -0.0625 to 0.0625
- w_down: bfloat16 [8, 2048, 7168], P('expert', 'dp'), may hold values from -0.125 to 0.125
Outputs:
- mixed_out: bfloat16 [128, 7168], P(('dp', 'expert'))
The draws below stay inside these ranges and needn't reach their ends.
Inputs may be any that keep to these rules, and one draw needn't show every extreme that they name: `routes`: each row names 2 different experts. In the rows of one device (aligned blocks of 4 rows) no expert is named by more than 2 rows, a bound that some block reaches.
All inputs are finite; a program needn't handle non-finite values.
Results may differ from the reference program's by a relative error of at most 0.0098.
Values may be sent and summed in bfloat16 or wider, within the bound.
A program may use at most 128 MiB of HBM per device.

```python
import math
import jax
import jax.numpy as jnp
import numpy as np
from jax import lax

D = 7168
FF = 2048
TOK_DEV = 4
EXPERTS = 8
TOP = 2
CAP = 2
TOKENS = 128
N_DP = 4
N_EXPERT = 8


def level_of(rng, shape, shards, least, top_value):
    loudness, own = 1.0, jax.random.fold_in(rng, 6)
    for axis_at, shards_of in shards:
        heights = jnp.exp(jax.random.uniform(jax.random.fold_in(own, axis_at), (shards_of,), jnp.float32, least / len(shards), top_value / len(shards)))
        loudness = loudness * jnp.repeat(heights, shape[axis_at] // shards_of).reshape([-1 if axis == axis_at else 1 for axis in range(len(shape))])
    return loudness


def assign_block(stream_key, own, number, rows, amount, top, limit, lean):
    ranking = jax.random.permutation(stream_key, amount)
    crowded, usual = portions_of(amount, rows * top, limit, lean, True), portions_of(amount, rows * top, limit, lean, False)
    places = jnp.arange(amount)

    def named(tallies, rotation):
        used = int((tallies > 0).sum())
        fixed = max(1, used // 4)
        passed = fixed + (places - fixed + rotation * (used - fixed)) % max(1, amount - fixed)
        return jnp.zeros((amount,), jnp.int32).at[ranking[jnp.where(places < fixed, places, passed)]].set(jnp.asarray(tallies, jnp.int32))

    tallies = jnp.where(number % 4 == 0, named(crowded, number // 4), named(usual, number - number // 4 - 1))
    mixed = jax.random.permutation(jax.random.fold_in(own, 3), amount)
    donor, receiver = mixed[0:amount // 2 * 2:2], mixed[1:amount // 2 * 2:2]
    slack = jnp.minimum(tallies[donor] - 1, limit - tallies[receiver]) // 2
    slack = jnp.where((donor == ranking[0]) | (receiver == ranking[0]) | (tallies[receiver] == 0), 0, jnp.maximum(slack, 0))
    passed = jax.random.randint(jax.random.fold_in(own, 4), (amount // 2,), 0, 1 << 20) % (slack + 1)
    tallies = tallies.at[donor].add(-passed).at[receiver].add(passed)
    items = jnp.searchsorted(jnp.cumsum(tallies), jnp.arange(rows * top), side="right").astype(jnp.int32)
    listing = items.reshape(top, rows).T
    listing = listing[jax.random.permutation(jax.random.fold_in(own, 1), rows)]
    rotation = jax.random.randint(jax.random.fold_in(own, 2), (rows, 1), 0, top)
    return jnp.take_along_axis(listing, (jnp.arange(top)[None, :] + rotation) % top, axis=1)


def portions_of(amount, total, most, lean, full):
    weights = [(1 << 20) // math.isqrt(standing ** lean) + 1 for standing in range(1, amount + 1)]
    largest = most if full else min(most, max(-(-total // amount), total * weights[0] // sum(weights)))
    least = 1 if total - largest >= amount - 1 else 0
    counts, rest = [largest] + [least] * (amount - 1), total - largest - least * (amount - 1)
    while rest > 0:
        free = [i for i in range(1, amount) if counts[i] < largest] or [i for i in range(1, amount) if counts[i] < most]
        mass, left = sum([weights[i] for i in free]), rest
        for i in free:
            extra = min(most - counts[i], max(1, left * weights[i] // mass), rest)
            counts[i] = counts[i] + extra
            rest = rest - extra
    return np.array(counts)


def scatter_about(rng, extent, width, reach, cuts=(), kind=jnp.bfloat16):
    gain = level_of(rng, extent, cuts, -0.22, 0.18) if cuts else 1.0
    values = jax.random.normal(rng, extent, jnp.float32) * width * gain
    return jnp.minimum(jnp.maximum(values, -reach), reach).astype(kind)


def setup_inputs(seed: int = 0) -> dict:
    keys = jax.random.split(jax.random.key(seed), 7)
    tokens = scatter_about(keys[0], (TOKENS, D), 1.0, 6.0, ((0, 32),))
    routes_keys = jax.random.split(jax.random.fold_in(keys[1], 1), TOKENS // TOK_DEV)
    routes_turns = jax.random.permutation(jax.random.fold_in(keys[1], 3), TOKENS // TOK_DEV)
    routes = jax.vmap(lambda own, number: assign_block(jax.random.fold_in(keys[1], 2), own, number, TOK_DEV, EXPERTS, TOP, CAP, 2))(routes_keys, routes_turns).reshape((TOKENS, TOP))
    gate_scores = jnp.clip(jnp.exp(math.log(1.0) - 2.3025851 * jax.random.uniform(keys[2], (TOKENS, TOP), jnp.float32) ** level_of(keys[2], (TOKENS, TOP), ((0, 32),), -0.2, 0.2)), 0.1, 1.0)
    w_gate = scatter_about(keys[3], (EXPERTS, D, FF), D ** -0.5, 0.0625, ((0, 8), (2, 4)))
    w_up = scatter_about(keys[4], (EXPERTS, D, FF), D ** -0.5, 0.0625, ((0, 8), (2, 4)))
    w_down = scatter_about(keys[5], (EXPERTS, FF, D), FF ** -0.5, 0.125, ((0, 8), (1, 4)))
    return dict(tokens=tokens, routes=routes, gate_scores=gate_scores, w_gate=w_gate, w_up=w_up, w_down=w_down)


def reference(tokens, routes, gate_scores, w_gate, w_up, w_down):
    token_count = tokens.shape[0]
    row_limit = min(token_count, N_DP * N_EXPERT * CAP)

    def one_expert(totals, inputs):
        expert_id, gate_mat, up_mat, down_mat = inputs
        matched = routes == expert_id
        chosen = jnp.any(matched, axis=1).astype(jnp.int32)
        route_weight = jnp.sum(jnp.where(matched, gate_scores, 0.0), axis=1)
        ranked = jnp.argsort(1 - chosen, stable=True)[:row_limit].astype(jnp.int32)
        picked_rows = tokens[ranked]
        gate_act = jnp.dot(picked_rows, gate_mat, preferred_element_type=jnp.float32)
        up_act = jnp.dot(picked_rows, up_mat, preferred_element_type=jnp.float32)
        hidden = (jax.nn.silu(gate_act) * up_act).astype(jnp.bfloat16)
        expert_out = jnp.dot(hidden, down_mat, preferred_element_type=jnp.float32)
        totals = totals.at[ranked].add(expert_out * route_weight[ranked][:, None])
        return totals, None

    numbers = jnp.arange(w_gate.shape[0], dtype=jnp.int32)
    start_sum = jnp.zeros(tokens.shape, jnp.float32)
    totals, _ = lax.scan(one_expert, start_sum, (numbers, w_gate, w_up, w_down))
    return totals.astype(jnp.bfloat16)
```

```python
import functools

import jax
import jax.numpy as jnp
from jax import lax
from jax.experimental import pallas as pl
from jax.experimental.pallas import tpu as pltpu
from jax.sharding import PartitionSpec as P

MESH = pl.DeviceIdType.MESH
F32, BF16 = jnp.float32, jnp.bfloat16


def divide(value, by):
    assert by & (by - 1) == 0
    return lax.shift_right_logical(value, jnp.int32(by.bit_length() - 1))


def modulo(value, by):
    assert by & (by - 1) == 0
    return lax.bitwise_and(value, jnp.int32(by - 1))


def kernel(
    sizes, tok, routes, scores, wg_hbm, wu_hbm, wd_hbm, out,
    wg, wu, wd, zbuf, mbuf, outg, arr, ret, back, sel_ref, comb_ref, gate, up, acc, zout, zin,
    wsem, zs, zr, ms, mr, ps, pr, rs, rr, os_, or_,
):
    groups, owners, rows, top, width, hidden, cap = sizes
    quarters = 16 // rows
    chunk = width // quarters
    per = groups * cap
    fold = max(1, 16 // per)
    tall = fold * per
    wide = width // fold
    parts = quarters // fold
    total, columns = owners * tall, groups * 16
    z, me = lax.axis_index("dp"), lax.axis_index("expert")

    def zpeer(i):
        return lax.rem(z + i, groups)

    def peer(i):
        return lax.rem(me + i, owners)

    barrier = pltpu.get_barrier_semaphore()

    @pl.loop(1, groups)
    def _(i):
        pl.semaphore_signal(barrier, inc=1, device_id=(zpeer(i), me), device_id_type=MESH)

    @pl.loop(1, owners)
    def _(i):
        pl.semaphore_signal(barrier, inc=1, device_id=(z, peer(i)), device_id_type=MESH)

    def weight_copies(p):
        for h in range(fold):
            span = pl.ds(h * wide + p * chunk, chunk)
            yield pltpu.make_async_copy(wg_hbm.at[0, span, :], wg.at[span, :], wsem.at[0, h, p])
            yield pltpu.make_async_copy(wu_hbm.at[0, span, :], wu.at[span, :], wsem.at[1, h, p])

    def down_copies(p):
        for h in range(fold):
            span = pl.ds(h * wide + p * chunk, chunk)
            yield pltpu.make_async_copy(wd_hbm.at[0, :, span], wd.at[:, span], wsem.at[2, h, p])

    for p in range(parts):
        for copy in weight_copies(p):
            copy.start()
    for p in range(parts):
        for copy in down_copies(p):
            copy.start()

    mine = tok[...].astype(F32)
    zbuf[z] = jnp.concatenate(
        [mine[:, q * chunk : (q + 1) * chunk] for q in range(quarters)], axis=0
    ).astype(BF16)
    pairs = rows * top
    for j in range(rows):
        for k in range(top):
            at = j * top + k
            mbuf[z, at : at + 1, :] = jnp.full((1, 128), routes[j, k], jnp.int32).astype(F32)
            mbuf[z, pairs + at : pairs + at + 1, :] = jnp.full((1, 128), scores[j, k], F32)

    pl.semaphore_wait(barrier, groups + owners - 2)

    def z_copy(block, to, of):
        return pltpu.make_async_remote_copy(
            zbuf.at[block], zbuf.at[block], zs.at[to], zr.at[of], (to, me), device_id_type=MESH)

    def m_copy(block, to, of):
        return pltpu.make_async_remote_copy(
            mbuf.at[block], mbuf.at[block], ms.at[to], mr.at[of], (to, me), device_id_type=MESH)

    @pl.loop(1, groups)
    def _(i):
        m_copy(z, zpeer(i), z).start()
        z_copy(z, zpeer(i), z).start()

    @pl.loop(1, groups)
    def _(i):
        m_copy(zpeer(i), zpeer(i), zpeer(i)).wait_recv()

    shape = (total, columns)
    r_at = lax.broadcasted_iota(jnp.int32, (total, 1), 0)
    c_at = lax.broadcasted_iota(jnp.int32, (1, columns), 1)
    e_r = divide(r_at, tall).astype(F32)
    h_r, z_r, s_r = divide(modulo(r_at, tall), per), divide(modulo(r_at, per), cap), modulo(r_at, cap)
    z_c, q_c, j_c = divide(c_at, 16), divide(modulo(c_at, 16), rows), modulo(c_at, rows)
    info = sum(
        jnp.where(z_c == g, mbuf[g][:, :columns], 0.0) for g in range(groups)
    )
    before = jnp.zeros(shape, F32)
    chosen = jnp.zeros(shape, F32)
    weight = jnp.zeros(shape, F32)
    for j in range(rows):
        match = jnp.zeros(shape, F32)
        score = jnp.zeros(shape, F32)
        for k in range(top):
            at = j * top + k
            same = info[at : at + 1, :] == e_r
            match = jnp.where(same, 1.0, match)
            score = jnp.where(same, info[pairs + at : pairs + at + 1, :], score)
        here = jnp.where((before == s_r.astype(F32)) & (j_c == j), match, 0.0)
        chosen = chosen + here
        weight = weight + here * score
        before = before + match
    for p in range(parts):
        fits = (z_r == z_c) & (q_c == h_r * parts + p)
        sel_ref[p] = jnp.where(fits, chosen, 0.0).astype(BF16)
        back_weight = jnp.transpose(jnp.where(fits, weight, 0.0))
        high = back_weight.astype(BF16)
        low = (back_weight - high.astype(F32)).astype(BF16)
        comb_ref[p] = jnp.concatenate([high, low], axis=0)

    @pl.loop(1, groups)
    def _(i):
        z_copy(zpeer(i), zpeer(i), zpeer(i)).wait_recv()

    def slots_copy(p, src, dst, to, of):
        span = pl.ds(p * chunk, chunk)
        return pltpu.make_async_remote_copy(
            outg.at[src, :, span], arr.at[dst, :, span], ps.at[p, to], pr.at[p, of],
            (z, to), device_id_type=MESH)

    tokens16 = zbuf[...].reshape(columns, chunk)
    for p in range(parts):
        span = pl.ds(p * chunk, chunk)
        picked = jnp.dot(sel_ref[p], tokens16, preferred_element_type=F32).astype(BF16)
        outg[:, :, span] = picked.reshape(owners, tall, chunk)

        @pl.loop(1, owners)
        def _(i, p=p):
            slots_copy(p, peer(i), me, peer(i), me).start()

        arr[me, :, span] = outg[me, :, span]

    some = min(owners, max(1, 128 // tall))
    blocks = owners // some
    for p in range(parts):
        span = pl.ds(p * chunk, chunk)
        for copy in weight_copies(p):
            copy.wait()

        @pl.loop(1, owners)
        def _(i, p=p):
            slots_copy(p, peer(i), peer(i), peer(i), peer(i)).wait_recv()

        @pl.loop(0, blocks)
        def _(b, p=p, span=span):
            first = b * some
            lhs = arr[pl.ds(first, some), :, span].reshape(some * tall, chunk)
            at = pl.ds(pl.multiple_of(first * per, some * per), some * per)
            for mat, into in ((wg, gate), (wu, up)):
                step = min(256, hidden)
                for n in range(0, hidden, step):
                    part = jnp.zeros((some, per, step), F32)
                    for h in range(fold):
                        res = jnp.dot(
                            lhs, mat[h * wide + p * chunk : h * wide + (p + 1) * chunk, n : n + step],
                            preferred_element_type=F32)
                        part = part + res.reshape(some, fold, per, step)[:, h]
                    part = part.reshape(some * per, step)
                    if p == 0:
                        into[at, n : n + step] = part
                    else:
                        into[at, n : n + step] += part

    def back_copy(p, src, dst, to, of):
        span = pl.ds(p * chunk, chunk)
        return pltpu.make_async_remote_copy(
            ret.at[src, :, span], back.at[dst, :, span], rs.at[p, to], rr.at[p, of],
            (z, to), device_id_type=MESH)

    for p in range(parts):
        span = pl.ds(p * chunk, chunk)
        for copy in down_copies(p):
            copy.wait()

        @pl.loop(0, blocks)
        def _(b, p=p):
            first = b * some
            at = pl.ds(pl.multiple_of(first * per, some * per), some * per)
            gate_act = gate[at, :]
            act = (gate_act / (1.0 + jnp.exp(-gate_act)) * up[at, :]).astype(BF16)
            step = 256
            for n in range(0, chunk, step):
                both = []
                for h in range(fold):
                    start = h * wide + p * chunk + n
                    res = jnp.dot(act, wd[:, start : start + step], preferred_element_type=F32)
                    both.append(res.reshape(some, per, step))
                ret[pl.ds(first, some), :, p * chunk + n : p * chunk + n + step] = jnp.concatenate(
                    both, axis=1).astype(BF16)

        @pl.loop(1, owners)
        def _(i, p=p):
            back_copy(p, peer(i), me, peer(i), me).start()

        back[me, :, span] = ret[me, :, span]

    for p in range(parts):
        @pl.loop(1, owners)
        def _(i, p=p):
            back_copy(p, peer(i), peer(i), peer(i), peer(i)).wait_recv()

        step = 256
        for n in range(0, chunk, step):
            rhs = back[:, :, p * chunk + n : p * chunk + n + step].reshape(total, step)
            res = jnp.dot(comb_ref[p], rhs, preferred_element_type=F32)
            res = res[:columns] + res[columns:]
            if p == 0:
                acc[:, n : n + step] = res
            else:
                acc[:, n : n + step] += res

    def sum_copy(src, dst, to, of):
        return pltpu.make_async_remote_copy(
            zout.at[src], zin.at[dst], os_.at[to], or_.at[of], (to, me), device_id_type=MESH)

    zout[...] = acc[...].astype(BF16).reshape(groups, 16, chunk)

    @pl.loop(1, groups)
    def _(i):
        sum_copy(zpeer(i), z, zpeer(i), z).start()

    own = acc[pl.ds(pl.multiple_of(z * 16, 16), 16), :]
    zin[z] = jnp.zeros((16, chunk), BF16)

    @pl.loop(1, groups)
    def _(i):
        sum_copy(zpeer(i), zpeer(i), zpeer(i), zpeer(i)).wait_recv()

    for g in range(groups):
        own = own + zin[g].astype(F32)
    for q in range(quarters):
        out[:, q * chunk : (q + 1) * chunk] = own[q * rows : (q + 1) * rows, :].astype(out.dtype)

    @pl.loop(1, groups)
    def _(i):
        m_copy(z, zpeer(i), z).wait_send()
        z_copy(z, zpeer(i), z).wait_send()
        sum_copy(zpeer(i), z, zpeer(i), z).wait_send()

    for p in range(parts):
        @pl.loop(1, owners)
        def _(i, p=p):
            slots_copy(p, peer(i), me, peer(i), me).wait_send()
            back_copy(p, peer(i), me, peer(i), me).wait_send()


def shards(tokens, routes, gate_scores, w_gate, w_up, w_down):
    rows, width = tokens.shape
    top = routes.shape[1]
    hidden = w_gate.shape[2]
    owners, groups = lax.axis_size("expert"), lax.axis_size("dp")
    cap = rows // 4 + 1
    quarters = 16 // rows
    chunk = width // quarters
    per = groups * cap
    fold = max(1, 16 // per)
    tall, wide, parts = fold * per, width // fold, quarters // fold
    total, columns = owners * tall, groups * 16
    sizes = (groups, owners, rows, top, width, hidden, cap)
    vmem = lambda shape, dtype=BF16: pltpu.VMEM(shape, dtype)
    dma = pltpu.SemaphoreType.DMA
    flops = 6 * owners * per * width * hidden
    return pl.pallas_call(
        functools.partial(kernel, sizes),
        out_shape=jax.ShapeDtypeStruct((rows, width), BF16),
        in_specs=[
            pl.BlockSpec(memory_space=pltpu.VMEM),
            pl.BlockSpec(memory_space=pltpu.SMEM),
            pl.BlockSpec(memory_space=pltpu.SMEM),
        ] + [pl.BlockSpec(memory_space=pl.ANY)] * 3,
        out_specs=pl.BlockSpec(memory_space=pltpu.VMEM),
        scratch_shapes=[
            vmem((width, hidden)), vmem((width, hidden)), vmem((hidden, width)),
            vmem((groups, 16, chunk)), vmem((groups, 2 * rows * top, 128), F32),
            vmem((owners, tall, wide)), vmem((owners, tall, wide)),
            vmem((owners, tall, wide)), vmem((owners, tall, wide)),
            vmem((parts, total, columns)), vmem((parts, 2 * columns, total)),
            vmem((owners * per, hidden), F32), vmem((owners * per, hidden), F32),
            vmem((columns, chunk), F32),
            vmem((groups, 16, chunk)), vmem((groups, 16, chunk)),
            dma((3, fold, parts)),
            dma((groups,)), dma((groups,)), dma((groups,)), dma((groups,)),
            dma((parts, owners)), dma((parts, owners)), dma((parts, owners)), dma((parts, owners)),
            dma((groups,)), dma((groups,)),
        ],
        compiler_params=pltpu.CompilerParams(
            collective_id=0, has_side_effects=True, vmem_limit_bytes=60 * 2**20),
        cost_estimate=pl.CostEstimate(
            flops=flops, bytes_accessed=6 * width * hidden, transcendentals=owners * per * hidden),
    )(tokens, routes, gate_scores, w_gate, w_up, w_down)


def solution(mesh):
    return jax.shard_map(
        shards,
        mesh=mesh,
        in_specs=(
            P(("dp", "expert"), None),
            P(("dp", "expert"), None),
            P(("dp", "expert"), None),
            P("expert", None, "dp"),
            P("expert", None, "dp"),
            P("expert", "dp", None),
        ),
        out_specs=P(("dp", "expert"), None),
        check_vma=False,
    )
```

```python
import functools

import jax
import jax.numpy as jnp
from jax import lax
from jax.experimental import pallas as pl
from jax.experimental.pallas import tpu as pltpu
from jax.sharding import PartitionSpec as P

MESH = pl.DeviceIdType.MESH
F32, BF16 = jnp.float32, jnp.bfloat16


def divide(value, by):
    assert by & (by - 1) == 0
    return lax.shift_right_logical(value, jnp.int32(by.bit_length() - 1))


def modulo(value, by):
    assert by & (by - 1) == 0
    return lax.bitwise_and(value, jnp.int32(by - 1))


def layout(sizes):
    groups, owners, rows, top, width, hidden, cap = sizes
    per = groups * cap
    fold = max(1, 16 // per)
    halves = 16 // (fold * rows)
    wide = width // fold
    small = 256 if wide % (halves * 256) == 0 else wide // halves
    chunk = halves * small
    return per, fold, fold * per, wide, halves, small, chunk, wide // chunk


def kernel(
    sizes, tok, routes, scores, wg_hbm, wu_hbm, wd_hbm, out,
    wg, wu, wd, zbuf, mbuf, outg, arr, ret, back, sel_ref, comb_ref, gate, up, act, acc, zout, zin,
    wsem, zs, zr, ms, mr, ps, pr, rs, rr, os_, or_,
):
    groups, owners, rows, top, width, hidden, cap = sizes
    per, fold, tall, wide, halves, small, chunk, parts = layout(sizes)
    total, columns = owners * tall, groups * 16
    z, me = lax.axis_index("dp"), lax.axis_index("expert")

    def zpeer(i):
        return lax.rem(z + i, groups)

    def peer(i):
        return lax.rem(me + i, owners)

    def span_of(p, base=0):
        return pl.ds(pl.multiple_of(base + p * chunk, chunk), chunk)

    barrier = pltpu.get_barrier_semaphore()

    @pl.loop(1, groups)
    def _(i):
        pl.semaphore_signal(barrier, inc=1, device_id=(zpeer(i), me), device_id_type=MESH)

    @pl.loop(1, owners)
    def _(i):
        pl.semaphore_signal(barrier, inc=1, device_id=(z, peer(i)), device_id_type=MESH)

    def weight_copies(p):
        for h in range(fold):
            span = span_of(p, h * wide)
            yield pltpu.make_async_copy(wg_hbm.at[0, span, :], wg.at[span, :], wsem.at[0, h, p])
            yield pltpu.make_async_copy(wu_hbm.at[0, span, :], wu.at[span, :], wsem.at[1, h, p])

    def down_copies(p):
        for h in range(fold):
            span = span_of(p, h * wide)
            yield pltpu.make_async_copy(wd_hbm.at[0, :, span], wd.at[:, span], wsem.at[2, h, p])

    mine = tok[...].astype(F32)
    for p in range(parts):
        pieces = []
        for h in range(fold):
            for u in range(halves):
                start = h * wide + p * chunk + u * small
                pieces.append(mine[:, start : start + small])
        zbuf[p, z] = jnp.concatenate(pieces, axis=0).astype(BF16)
    pairs = rows * top
    for j in range(rows):
        for k in range(top):
            at = j * top + k
            mbuf[z, at : at + 1, :] = jnp.full((1, 128), routes[k, j], jnp.int32).astype(F32)
            mbuf[z, pairs + at : pairs + at + 1, :] = jnp.full((1, 128), scores[k, j], F32)

    pl.semaphore_wait(barrier, groups + owners - 2)

    def z_copy(p, block, to, of):
        return pltpu.make_async_remote_copy(
            zbuf.at[p, block], zbuf.at[p, block], zs.at[p, to], zr.at[p, of],
            (to, me), device_id_type=MESH)

    def m_copy(block, to, of):
        return pltpu.make_async_remote_copy(
            mbuf.at[block], mbuf.at[block], ms.at[to], mr.at[of], (to, me), device_id_type=MESH)

    @pl.loop(1, groups)
    def _(i):
        m_copy(z, zpeer(i), z).start()

    @pl.loop(0, parts)
    def _(p):
        @pl.loop(1, groups)
        def _(i):
            z_copy(p, z, zpeer(i), z).start()

    @pl.loop(0, parts)
    def _(p):
        for copy in weight_copies(p):
            copy.start()

    @pl.loop(0, parts)
    def _(p):
        for copy in down_copies(p):
            copy.start()

    gate[...] = jnp.zeros_like(gate)
    up[...] = jnp.zeros_like(up)

    @pl.loop(1, groups)
    def _(i):
        m_copy(zpeer(i), zpeer(i), zpeer(i)).wait_recv()

    shape = (total, columns)
    r_at = lax.broadcasted_iota(jnp.int32, (total, 1), 0)
    c_at = lax.broadcasted_iota(jnp.int32, (1, columns), 1)
    e_r = divide(r_at, tall).astype(F32)
    h_r, z_r, s_r = divide(modulo(r_at, tall), per), divide(modulo(r_at, per), cap), modulo(r_at, cap)
    z_c, q_c, j_c = divide(c_at, 16), divide(modulo(c_at, 16), rows), modulo(c_at, rows)
    info = sum(
        jnp.where(z_c == g, mbuf[g][:, :columns], 0.0) for g in range(groups)
    )
    before = jnp.zeros(shape, F32)
    chosen = jnp.zeros(shape, F32)
    weight = jnp.zeros(shape, F32)
    for j in range(rows):
        match = jnp.zeros(shape, F32)
        score = jnp.zeros(shape, F32)
        for k in range(top):
            at = j * top + k
            same = info[at : at + 1, :] == e_r
            match = jnp.where(same, 1.0, match)
            score = jnp.where(same, info[pairs + at : pairs + at + 1, :], score)
        here = jnp.where((before == s_r.astype(F32)) & (j_c == j), match, 0.0)
        chosen = chosen + here
        weight = weight + here * score
        before = before + match
    for u in range(halves):
        fits = (z_r == z_c) & (q_c == h_r * halves + u)
        sel_ref[u] = jnp.where(fits, chosen, 0.0).astype(BF16)
        back_weight = jnp.transpose(jnp.where(fits, weight, 0.0))
        high = back_weight.astype(BF16)
        low = (back_weight - high.astype(F32)).astype(BF16)
        comb_ref[u] = jnp.concatenate([high, low], axis=0)

    def slots_copy(p, src, dst, to, of):
        span = span_of(p)
        return pltpu.make_async_remote_copy(
            outg.at[src, :, span], arr.at[dst, :, span], ps.at[p, to], pr.at[p, of],
            (z, to), device_id_type=MESH)

    @pl.loop(0, parts)
    def _(p):
        @pl.loop(1, groups)
        def _(i):
            z_copy(p, zpeer(i), zpeer(i), zpeer(i)).wait_recv()

        tokens16 = zbuf[p].reshape(columns, small)
        for u in range(halves):
            picked = jnp.dot(sel_ref[u], tokens16, preferred_element_type=F32).astype(BF16)
            outg[:, :, pl.ds(pl.multiple_of(p * chunk + u * small, small), small)] = picked.reshape(
                owners, tall, small)

        @pl.loop(1, owners)
        def _(i):
            slots_copy(p, peer(i), me, peer(i), me).start()

        arr[me, :, span_of(p)] = outg[me, :, span_of(p)]

    some = min(owners, max(1, 128 // tall))
    blocks = owners // some

    @pl.loop(0, parts)
    def _(p):
        for copy in weight_copies(p):
            copy.wait()

        @pl.loop(1, owners)
        def _(i):
            slots_copy(p, peer(i), peer(i), peer(i), peer(i)).wait_recv()

        @pl.loop(0, blocks)
        def _(b):
            first = b * some
            lhs = arr[pl.ds(first, some), :, span_of(p)].reshape(some * tall, chunk)
            at = pl.ds(pl.multiple_of(first * per, some * per), some * per)
            step = min(256, hidden)
            for mat, into in ((wg, gate), (wu, up)):
                for n in range(0, hidden, step):
                    part = into[at, n : n + step].reshape(some, per, step)
                    for h in range(fold):
                        res = jnp.dot(
                            lhs, mat[span_of(p, h * wide), n : n + step],
                            preferred_element_type=F32)
                        part = part + res.reshape(some, fold, per, step)[:, h]
                    into[at, n : n + step] = part.reshape(some * per, step)

    gate_act = gate[...]
    act[...] = (gate_act / (1.0 + jnp.exp(-gate_act)) * up[...]).astype(BF16)

    def back_copy(p, src, dst, to, of):
        span = span_of(p)
        return pltpu.make_async_remote_copy(
            ret.at[src, :, span], back.at[dst, :, span], rs.at[p, to], rr.at[p, of],
            (z, to), device_id_type=MESH)

    @pl.loop(0, parts)
    def _(p):
        for copy in down_copies(p):
            copy.wait()

        @pl.loop(0, blocks)
        def _(b):
            first = b * some
            at = pl.ds(pl.multiple_of(first * per, some * per), some * per)
            lhs = act[at, :]
            both = [
                jnp.dot(lhs, wd[:, span_of(p, h * wide)], preferred_element_type=F32).reshape(
                    some, per, chunk)
                for h in range(fold)
            ]
            ret[pl.ds(first, some), :, span_of(p)] = jnp.concatenate(both, axis=1).astype(BF16)

        @pl.loop(1, owners)
        def _(i):
            back_copy(p, peer(i), me, peer(i), me).start()

        back[me, :, span_of(p)] = ret[me, :, span_of(p)]

    def sum_copy(p, src, dst, to, of):
        return pltpu.make_async_remote_copy(
            zout.at[p, src], zin.at[p, dst], os_.at[p, to], or_.at[p, of],
            (to, me), device_id_type=MESH)

    @pl.loop(0, parts)
    def _(p):
        @pl.loop(1, owners)
        def _(i):
            back_copy(p, peer(i), peer(i), peer(i), peer(i)).wait_recv()

        mixed = jnp.zeros((columns, small), F32)
        for u in range(halves):
            rhs = back[:, :, pl.ds(pl.multiple_of(p * chunk + u * small, small), small)]
            res = jnp.dot(comb_ref[u], rhs.reshape(total, small), preferred_element_type=F32)
            mixed = mixed + res[:columns] + res[columns:]
        acc[p] = mixed
        zout[p] = mixed.astype(BF16).reshape(groups, 16, small)

        @pl.loop(1, groups)
        def _(i):
            sum_copy(p, zpeer(i), z, zpeer(i), z).start()

        zin[p, z] = jnp.zeros((16, small), BF16)

    for p in range(parts):
        @pl.loop(1, groups)
        def _(i, p=p):
            sum_copy(p, zpeer(i), zpeer(i), zpeer(i), zpeer(i)).wait_recv()

        own = acc[p, pl.ds(pl.multiple_of(z * 16, 16), 16), :]
        for g in range(groups):
            own = own + zin[p, g].astype(F32)
        for h in range(fold):
            for u in range(halves):
                start, row = h * wide + p * chunk + u * small, (h * halves + u) * rows
                out[:, start : start + small] = own[row : row + rows, :].astype(out.dtype)

    @pl.loop(1, groups)
    def _(i):
        m_copy(z, zpeer(i), z).wait_send()

    @pl.loop(0, parts)
    def _(p):
        @pl.loop(1, groups)
        def _(i):
            z_copy(p, z, zpeer(i), z).wait_send()
            sum_copy(p, zpeer(i), z, zpeer(i), z).wait_send()

        @pl.loop(1, owners)
        def _(i):
            slots_copy(p, peer(i), me, peer(i), me).wait_send()
            back_copy(p, peer(i), me, peer(i), me).wait_send()


def shards(tokens, routes, gate_scores, w_gate, w_up, w_down):
    rows, width = tokens.shape
    top = routes.shape[1]
    hidden = w_gate.shape[2]
    owners, groups = lax.axis_size("expert"), lax.axis_size("dp")
    cap = rows // 4 + 1
    sizes = (groups, owners, rows, top, width, hidden, cap)
    per, fold, tall, wide, halves, small, chunk, parts = layout(sizes)
    total, columns = owners * tall, groups * 16
    vmem = lambda shape, dtype=BF16: pltpu.VMEM(shape, dtype)
    dma = pltpu.SemaphoreType.DMA
    flops = 6 * owners * per * width * hidden
    return pl.pallas_call(
        functools.partial(kernel, sizes),
        out_shape=jax.ShapeDtypeStruct((rows, width), BF16),
        in_specs=[
            pl.BlockSpec(memory_space=pltpu.VMEM),
            pl.BlockSpec(memory_space=pltpu.SMEM),
            pl.BlockSpec(memory_space=pltpu.SMEM),
        ] + [pl.BlockSpec(memory_space=pl.ANY)] * 3,
        out_specs=pl.BlockSpec(memory_space=pltpu.VMEM),
        scratch_shapes=[
            vmem((width, hidden)), vmem((width, hidden)), vmem((hidden, width)),
            vmem((parts, groups, 16, small)), vmem((groups, 2 * rows * top, 128), F32),
            vmem((owners, tall, wide)), vmem((owners, tall, wide)),
            vmem((owners, tall, wide)), vmem((owners, tall, wide)),
            vmem((halves, total, columns)), vmem((halves, 2 * columns, total)),
            vmem((owners * per, hidden), F32), vmem((owners * per, hidden), F32),
            vmem((owners * per, hidden)), vmem((parts, columns, small), F32),
            vmem((parts, groups, 16, small)), vmem((parts, groups, 16, small)),
            dma((3, fold, parts)),
            dma((parts, groups)), dma((parts, groups)), dma((groups,)), dma((groups,)),
            dma((parts, owners)), dma((parts, owners)), dma((parts, owners)), dma((parts, owners)),
            dma((parts, groups)), dma((parts, groups)),
        ],
        compiler_params=pltpu.CompilerParams(
            collective_id=0, has_side_effects=True, vmem_limit_bytes=60 * 2**20),
        cost_estimate=pl.CostEstimate(
            flops=flops, bytes_accessed=6 * width * hidden, transcendentals=owners * per * hidden),
    )(tokens, routes.T, gate_scores.T, w_gate, w_up, w_down)


def solution(mesh):
    return jax.shard_map(
        shards,
        mesh=mesh,
        in_specs=(
            P(("dp", "expert"), None),
            P(("dp", "expert"), None),
            P(("dp", "expert"), None),
            P("expert", None, "dp"),
            P("expert", None, "dp"),
            P("expert", "dp", None),
        ),
        out_specs=P(("dp", "expert"), None),
        check_vma=False,
    )
```

```python
import functools

import jax
import jax.numpy as jnp
from jax import lax
from jax.experimental import pallas as pl
from jax.experimental.pallas import tpu as pltpu
from jax.sharding import PartitionSpec as P

MESH = pl.DeviceIdType.MESH
F32, BF16 = jnp.float32, jnp.bfloat16


def divide(value, by):
    assert by & (by - 1) == 0
    return lax.shift_right_logical(value, jnp.int32(by.bit_length() - 1))


def modulo(value, by):
    assert by & (by - 1) == 0
    return lax.bitwise_and(value, jnp.int32(by - 1))


def layout(sizes):
    groups, owners, rows, top, width, hidden, cap = sizes
    per = groups * cap
    fold = max(1, 16 // per)
    halves = 16 // (fold * rows)
    wide = width // fold
    small = 256 if wide % (halves * 256) == 0 else wide // halves
    chunk = halves * small
    return per, fold, fold * per, wide, halves, small, chunk, wide // chunk


def kernel(
    sizes, tok, routes, scores, wg_hbm, wu_hbm, wd_hbm, out,
    wg, wu, wd, zbuf, mbuf, outg, arr, ret, back, sel_ref, comb_ref, gate, up, act, acc, zout, zin,
    wsem, zs, zr, ms, mr, ps, pr, rs, rr, os_, or_,
):
    groups, owners, rows, top, width, hidden, cap = sizes
    per, fold, tall, wide, halves, small, chunk, parts = layout(sizes)
    total, columns = owners * tall, groups * 16
    z, me = lax.axis_index("dp"), lax.axis_index("expert")

    zpeers = [modulo(z + i, groups) for i in range(1, groups)]
    peers = [modulo(me + i, owners) for i in range(1, owners)]

    def span_of(p, base=0):
        return pl.ds(pl.multiple_of(base + p * chunk, chunk), chunk)

    barrier = pltpu.get_barrier_semaphore()

    for to in zpeers:
        pl.semaphore_signal(barrier, inc=1, device_id=(to, me), device_id_type=MESH)
    for to in peers:
        pl.semaphore_signal(barrier, inc=1, device_id=(z, to), device_id_type=MESH)

    def arrive(ref, sem):
        pltpu.make_async_copy(ref, ref, sem).wait()

    mine = tok[...].astype(F32)
    for p in range(parts):
        pieces = []
        for h in range(fold):
            for u in range(halves):
                start = h * wide + p * chunk + u * small
                pieces.append(mine[:, start : start + small])
        zbuf[p, z] = jnp.concatenate(pieces, axis=0).astype(BF16)
    pairs = rows * top
    for j in range(rows):
        for k in range(top):
            at = j * top + k
            mbuf[z, at : at + 1, :] = jnp.full((1, 128), routes[k, j], jnp.int32).astype(F32)
            mbuf[z, pairs + at : pairs + at + 1, :] = jnp.full((1, 128), scores[k, j], F32)

    pl.semaphore_wait(barrier, groups + owners - 2)

    for to in zpeers:
        pltpu.make_async_remote_copy(
            mbuf.at[z], mbuf.at[z], ms, mr, (to, me), device_id_type=MESH).start()
    for p in range(parts):
        for to in zpeers:
            pltpu.make_async_remote_copy(
                zbuf.at[p, z], zbuf.at[p, z], zs, zr.at[p], (to, me), device_id_type=MESH).start()
    for at, (src, dst) in enumerate(((wg_hbm, wg), (wu_hbm, wu), (wd_hbm, wd))):
        piece = dst.shape[0] // 4
        for i in range(4):
            span = pl.ds(i * piece, piece)
            pltpu.make_async_copy(src.at[0, span, :], dst.at[span, :], wsem.at[at]).start()

    gate[...] = jnp.zeros_like(gate)
    up[...] = jnp.zeros_like(up)

    arrive(mbuf.at[pl.ds(0, groups - 1)], mr)

    shape = (total, columns)
    r_at = lax.broadcasted_iota(jnp.int32, (total, 1), 0)
    c_at = lax.broadcasted_iota(jnp.int32, (1, columns), 1)
    e_r = divide(r_at, tall).astype(F32)
    h_r, z_r, s_r = divide(modulo(r_at, tall), per), divide(modulo(r_at, per), cap), modulo(r_at, cap)
    z_c, q_c, j_c = divide(c_at, 16), divide(modulo(c_at, 16), rows), modulo(c_at, rows)
    info = sum(
        jnp.where(z_c == g, mbuf[g][:, :columns], 0.0) for g in range(groups)
    )
    before = jnp.zeros(shape, F32)
    chosen = jnp.zeros(shape, F32)
    weight = jnp.zeros(shape, F32)
    for j in range(rows):
        match = jnp.zeros(shape, F32)
        score = jnp.zeros(shape, F32)
        for k in range(top):
            at = j * top + k
            same = info[at : at + 1, :] == e_r
            match = jnp.where(same, 1.0, match)
            score = jnp.where(same, info[pairs + at : pairs + at + 1, :], score)
        here = jnp.where((before == s_r.astype(F32)) & (j_c == j), match, 0.0)
        chosen = chosen + here
        weight = weight + here * score
        before = before + match
    for u in range(halves):
        fits = (z_r == z_c) & (q_c == h_r * halves + u)
        sel_ref[u] = jnp.where(fits, chosen, 0.0).astype(BF16)
        back_weight = jnp.transpose(jnp.where(fits, weight, 0.0))
        high = back_weight.astype(BF16)
        low = (back_weight - high.astype(F32)).astype(BF16)
        comb_ref[u] = jnp.concatenate([high, low], axis=0)

    @pl.loop(0, parts)
    def _(p):
        arrive(zbuf.at[p, pl.ds(0, groups - 1)], zr.at[p])
        tokens16 = zbuf[p].reshape(columns, small)
        for u in range(halves):
            picked = jnp.dot(sel_ref[u], tokens16, preferred_element_type=F32).astype(BF16)
            outg[:, :, pl.ds(pl.multiple_of(p * chunk + u * small, small), small)] = picked.reshape(
                owners, tall, small)

        span = span_of(p)
        for to in peers:
            pltpu.make_async_remote_copy(
                outg.at[to, :, span], arr.at[me, :, span], ps, pr.at[p],
                (z, to), device_id_type=MESH).start()

        arr[me, :, span_of(p)] = outg[me, :, span_of(p)]

    some = min(owners, max(1, 128 // tall))
    blocks = owners // some

    arrive(wg, wsem.at[0])
    arrive(wu, wsem.at[1])

    @pl.loop(0, parts)
    def _(p):
        arrive(arr.at[pl.ds(0, owners - 1), :, span_of(p)], pr.at[p])

        @pl.loop(0, blocks)
        def _(b):
            first = b * some
            lhs = arr[pl.ds(first, some), :, span_of(p)].reshape(some * tall, chunk)
            at = pl.ds(pl.multiple_of(first * per, some * per), some * per)
            step = min(256, hidden)
            for mat, into in ((wg, gate), (wu, up)):
                for n in range(0, hidden, step):
                    part = into[at, n : n + step].reshape(some, per, step)
                    for h in range(fold):
                        res = jnp.dot(
                            lhs, mat[span_of(p, h * wide), n : n + step],
                            preferred_element_type=F32)
                        part = part + res.reshape(some, fold, per, step)[:, h]
                    into[at, n : n + step] = part.reshape(some * per, step)

    gate_act = gate[...]
    act[...] = (gate_act / (1.0 + jnp.exp(-gate_act)) * up[...]).astype(BF16)

    arrive(wd, wsem.at[2])

    @pl.loop(0, parts)
    def _(p):
        @pl.loop(0, blocks)
        def _(b):
            first = b * some
            at = pl.ds(pl.multiple_of(first * per, some * per), some * per)
            lhs = act[at, :]
            both = [
                jnp.dot(lhs, wd[:, span_of(p, h * wide)], preferred_element_type=F32).reshape(
                    some, per, chunk)
                for h in range(fold)
            ]
            ret[pl.ds(first, some), :, span_of(p)] = jnp.concatenate(both, axis=1).astype(BF16)

        span = span_of(p)
        for to in peers:
            pltpu.make_async_remote_copy(
                ret.at[to, :, span], back.at[me, :, span], rs, rr.at[p],
                (z, to), device_id_type=MESH).start()

        back[me, :, span_of(p)] = ret[me, :, span_of(p)]

    arrive(mbuf.at[pl.ds(0, groups - 1)], ms)
    arrive(zbuf.at[:, pl.ds(0, groups - 1)], zs)
    arrive(outg.at[pl.ds(0, owners - 1)], ps)

    @pl.loop(0, parts)
    def _(p):
        arrive(back.at[pl.ds(0, owners - 1), :, span_of(p)], rr.at[p])
        mixed = jnp.zeros((columns, small), F32)
        for u in range(halves):
            rhs = back[:, :, pl.ds(pl.multiple_of(p * chunk + u * small, small), small)]
            res = jnp.dot(comb_ref[u], rhs.reshape(total, small), preferred_element_type=F32)
            mixed = mixed + res[:columns] + res[columns:]
        acc[p] = mixed
        zout[p] = mixed.astype(BF16).reshape(groups, 16, small)

        for to in zpeers:
            pltpu.make_async_remote_copy(
                zout.at[p, to], zin.at[p, z], os_, or_.at[p], (to, me), device_id_type=MESH).start()

        zin[p, z] = jnp.zeros((16, small), BF16)

    arrive(ret.at[pl.ds(0, owners - 1)], rs)
    for p in range(parts):
        arrive(zin.at[p, pl.ds(0, groups - 1)], or_.at[p])
        own = acc[p, pl.ds(pl.multiple_of(z * 16, 16), 16), :]
        for g in range(groups):
            own = own + zin[p, g].astype(F32)
        for h in range(fold):
            for u in range(halves):
                start, row = h * wide + p * chunk + u * small, (h * halves + u) * rows
                out[:, start : start + small] = own[row : row + rows, :].astype(out.dtype)

    arrive(zout.at[:, pl.ds(0, groups - 1)], os_)


def shards(tokens, routes, gate_scores, w_gate, w_up, w_down):
    rows, width = tokens.shape
    top = routes.shape[1]
    hidden = w_gate.shape[2]
    owners, groups = lax.axis_size("expert"), lax.axis_size("dp")
    cap = rows // 4 + 1
    sizes = (groups, owners, rows, top, width, hidden, cap)
    per, fold, tall, wide, halves, small, chunk, parts = layout(sizes)
    total, columns = owners * tall, groups * 16
    vmem = lambda shape, dtype=BF16: pltpu.VMEM(shape, dtype)
    dma = pltpu.SemaphoreType.DMA
    flops = 6 * owners * per * width * hidden
    return pl.pallas_call(
        functools.partial(kernel, sizes),
        out_shape=jax.ShapeDtypeStruct((rows, width), BF16),
        in_specs=[
            pl.BlockSpec(memory_space=pltpu.VMEM),
            pl.BlockSpec(memory_space=pltpu.SMEM),
            pl.BlockSpec(memory_space=pltpu.SMEM),
        ] + [pl.BlockSpec(memory_space=pl.ANY)] * 3,
        out_specs=pl.BlockSpec(memory_space=pltpu.VMEM),
        scratch_shapes=[
            vmem((width, hidden)), vmem((width, hidden)), vmem((hidden, width)),
            vmem((parts, groups, 16, small)), vmem((groups, 2 * rows * top, 128), F32),
            vmem((owners, tall, wide)), vmem((owners, tall, wide)),
            vmem((owners, tall, wide)), vmem((owners, tall, wide)),
            vmem((halves, total, columns)), vmem((halves, 2 * columns, total)),
            vmem((owners * per, hidden), F32), vmem((owners * per, hidden), F32),
            vmem((owners * per, hidden)), vmem((parts, columns, small), F32),
            vmem((parts, groups, 16, small)), vmem((parts, groups, 16, small)),
            dma((3,)), dma, dma((parts,)), dma, dma,
            dma, dma((parts,)), dma, dma((parts,)), dma, dma((parts,)),
        ],
        compiler_params=pltpu.CompilerParams(
            collective_id=0, has_side_effects=True, vmem_limit_bytes=60 * 2**20),
        cost_estimate=pl.CostEstimate(
            flops=flops, bytes_accessed=6 * width * hidden, transcendentals=owners * per * hidden),
    )(tokens, routes.T, gate_scores.T, w_gate, w_up, w_down)


def solution(mesh):
    return jax.shard_map(
        shards,
        mesh=mesh,
        in_specs=(
            P(("dp", "expert"), None),
            P(("dp", "expert"), None),
            P(("dp", "expert"), None),
            P("expert", None, "dp"),
            P("expert", None, "dp"),
            P("expert", "dp", None),
        ),
        out_specs=P(("dp", "expert"), None),
        check_vma=False,
    )
```

```python
import functools

import jax
import jax.numpy as jnp
from jax import lax
from jax.experimental import pallas as pl
from jax.experimental.pallas import tpu as pltpu
from jax.sharding import PartitionSpec as P

MESH = pl.DeviceIdType.MESH
F32, BF16 = jnp.float32, jnp.bfloat16


def divide(value, by):
    assert by & (by - 1) == 0
    return lax.shift_right_logical(value, jnp.int32(by.bit_length() - 1))


def modulo(value, by):
    assert by & (by - 1) == 0
    return lax.bitwise_and(value, jnp.int32(by - 1))


def layout(sizes):
    groups, owners, rows, top, width, hidden, cap = sizes
    per = groups * cap
    fold = max(1, 16 // per)
    halves = 16 // (fold * rows)
    wide = width // fold
    small = 256 if wide % (halves * 256) == 0 else wide // halves
    chunk = halves * small
    return per, fold, fold * per, wide, halves, small, chunk, wide // chunk


def kernel(
    sizes, tok, routes, scores, wg_hbm, wu_hbm, wd_hbm, out,
    wg, wu, wd, zbuf, mbuf, outg, arr, ret, back, sel_ref, comb_ref, gate, up, act, acc, zout, zin,
    wsem, zs, zr, ms, mr, ps, pr, rs, rr, os_, or_,
):
    groups, owners, rows, top, width, hidden, cap = sizes
    per, fold, tall, wide, halves, small, chunk, parts = layout(sizes)
    total, columns = owners * tall, groups * 16
    z, me = lax.axis_index("dp"), lax.axis_index("expert")

    zpeers = [modulo(z + i, groups) for i in range(1, groups)]
    peers = [modulo(me + i, owners) for i in (*range(2, owners - 1), 1, owners - 1)]

    def span_of(p, base=0):
        return pl.ds(pl.multiple_of(base + p * chunk, chunk), chunk)

    barrier = pltpu.get_barrier_semaphore()

    for to in zpeers:
        pl.semaphore_signal(barrier, inc=1, device_id=(to, me), device_id_type=MESH)
    for to in peers:
        pl.semaphore_signal(barrier, inc=1, device_id=(z, to), device_id_type=MESH)

    def arrive(ref, sem):
        pltpu.make_async_copy(ref, ref, sem).wait()

    for at, (src, dst) in enumerate(((wg_hbm, wg), (wu_hbm, wu), (wd_hbm, wd))):
        piece = dst.shape[0] // 4
        for i in range(4):
            span = pl.ds(i * piece, piece)
            pltpu.make_async_copy(src.at[0, span, :], dst.at[span, :], wsem.at[at]).start()

    mine = tok[...].astype(F32)
    for p in range(parts):
        pieces = []
        for h in range(fold):
            for u in range(halves):
                start = h * wide + p * chunk + u * small
                pieces.append(mine[:, start : start + small])
        zbuf[p, z] = jnp.concatenate(pieces, axis=0).astype(BF16)
    pairs = rows * top
    for j in range(rows):
        for k in range(top):
            at = j * top + k
            mbuf[z, at : at + 1, :] = jnp.full((1, 128), routes[k, j], jnp.int32).astype(F32)
            mbuf[z, pairs + at : pairs + at + 1, :] = jnp.full((1, 128), scores[k, j], F32)

    pl.semaphore_wait(barrier, groups + owners - 2)

    for to in zpeers:
        pltpu.make_async_remote_copy(
            mbuf.at[z], mbuf.at[z], ms, mr, (to, me), device_id_type=MESH).start()
    for p in range(parts):
        for to in zpeers:
            pltpu.make_async_remote_copy(
                zbuf.at[p, z], zbuf.at[p, z], zs, zr.at[p], (to, me), device_id_type=MESH).start()
    gate[...] = jnp.zeros_like(gate)
    up[...] = jnp.zeros_like(up)

    arrive(mbuf.at[pl.ds(0, groups - 1)], mr)

    shape = (total, columns)
    r_at = lax.broadcasted_iota(jnp.int32, (total, 1), 0)
    c_at = lax.broadcasted_iota(jnp.int32, (1, columns), 1)
    e_r = divide(r_at, tall).astype(F32)
    h_r, z_r, s_r = divide(modulo(r_at, tall), per), divide(modulo(r_at, per), cap), modulo(r_at, cap)
    z_c, q_c, j_c = divide(c_at, 16), divide(modulo(c_at, 16), rows), modulo(c_at, rows)
    info = sum(
        jnp.where(z_c == g, mbuf[g][:, :columns], 0.0) for g in range(groups)
    )
    before = jnp.zeros(shape, F32)
    chosen = jnp.zeros(shape, F32)
    weight = jnp.zeros(shape, F32)
    for j in range(rows):
        match = jnp.zeros(shape, F32)
        score = jnp.zeros(shape, F32)
        for k in range(top):
            at = j * top + k
            same = info[at : at + 1, :] == e_r
            match = jnp.where(same, 1.0, match)
            score = jnp.where(same, info[pairs + at : pairs + at + 1, :], score)
        here = jnp.where((before == s_r.astype(F32)) & (j_c == j), match, 0.0)
        chosen = chosen + here
        weight = weight + here * score
        before = before + match
    for u in range(halves):
        fits = (z_r == z_c) & (q_c == h_r * halves + u)
        sel_ref[u] = jnp.where(fits, chosen, 0.0).astype(BF16)

    @pl.loop(0, parts)
    def _(p):
        arrive(zbuf.at[p, pl.ds(0, groups - 1)], zr.at[p])
        tokens16 = zbuf[p].reshape(columns, small)
        for u in range(halves):
            picked = jnp.dot(sel_ref[u], tokens16, preferred_element_type=F32).astype(BF16)
            outg[p, :, :, u * small : (u + 1) * small] = picked.reshape(
                owners, tall, small)

        for to in peers:
            pltpu.make_async_remote_copy(
                outg.at[p, to], arr.at[p, me], ps, pr.at[p],
                (z, to), device_id_type=MESH).start()

        arr[p, me] = outg[p, me]

    for u in range(halves):
        fits = (z_r == z_c) & (q_c == h_r * halves + u)
        back_weight = jnp.transpose(jnp.where(fits, weight, 0.0))
        high = back_weight.astype(BF16)
        low = (back_weight - high.astype(F32)).astype(BF16)
        comb_ref[u] = jnp.concatenate([high, low], axis=0)

    some = min(owners, max(1, 128 // tall))
    blocks = owners // some

    arrive(wg, wsem.at[0])
    arrive(wu, wsem.at[1])

    @pl.loop(0, parts)
    def _(p):
        arrive(arr.at[p, pl.ds(0, owners - 1)], pr.at[p])

        @pl.loop(0, blocks)
        def _(b):
            first = b * some
            lhs = arr[p, pl.ds(first, some)].reshape(some * tall, chunk)
            at = pl.ds(pl.multiple_of(first * per, some * per), some * per)
            step = min(256, hidden)
            for mat, into in ((wg, gate), (wu, up)):
                for n in range(0, hidden, step):
                    part = into[at, n : n + step].reshape(some, per, step)
                    for h in range(fold):
                        res = jnp.dot(
                            lhs, mat[span_of(p, h * wide), n : n + step],
                            preferred_element_type=F32)
                        part = part + res.reshape(some, fold, per, step)[:, h]
                    into[at, n : n + step] = part.reshape(some * per, step)

    gate_act = gate[...]
    act[...] = (gate_act / (1.0 + jnp.exp(-gate_act)) * up[...]).astype(BF16)

    arrive(wd, wsem.at[2])

    @pl.loop(0, parts)
    def _(p):
        @pl.loop(0, blocks)
        def _(b):
            first = b * some
            at = pl.ds(pl.multiple_of(first * per, some * per), some * per)
            lhs = act[at, :]
            both = [
                jnp.dot(lhs, wd[:, span_of(p, h * wide)], preferred_element_type=F32).reshape(
                    some, per, chunk)
                for h in range(fold)
            ]
            ret[p, pl.ds(first, some)] = jnp.concatenate(both, axis=1).astype(BF16)

        for to in peers:
            pltpu.make_async_remote_copy(
                ret.at[p, to], back.at[p, me], rs, rr.at[p],
                (z, to), device_id_type=MESH).start()

        back[p, me] = ret[p, me]

    arrive(mbuf.at[pl.ds(0, groups - 1)], ms)
    arrive(zbuf.at[:, pl.ds(0, groups - 1)], zs)
    arrive(outg.at[:, pl.ds(0, owners - 1)], ps)

    @pl.loop(0, parts)
    def _(p):
        arrive(back.at[p, pl.ds(0, owners - 1)], rr.at[p])
        mixed = jnp.zeros((columns, small), F32)
        for u in range(halves):
            rhs = back[p, :, :, u * small : (u + 1) * small]
            res = jnp.dot(comb_ref[u], rhs.reshape(total, small), preferred_element_type=F32)
            mixed = mixed + res[:columns] + res[columns:]
        acc[p] = mixed
        zout[p] = mixed.astype(BF16).reshape(groups, 16, small)

        for to in zpeers:
            pltpu.make_async_remote_copy(
                zout.at[p, to], zin.at[p, z], os_, or_.at[p], (to, me), device_id_type=MESH).start()

        zin[p, z] = jnp.zeros((16, small), BF16)

    arrive(ret.at[:, pl.ds(0, owners - 1)], rs)
    for p in range(parts):
        arrive(zin.at[p, pl.ds(0, groups - 1)], or_.at[p])
        own = acc[p, pl.ds(pl.multiple_of(z * 16, 16), 16), :]
        for g in range(groups):
            own = own + zin[p, g].astype(F32)
        for h in range(fold):
            for u in range(halves):
                start, row = h * wide + p * chunk + u * small, (h * halves + u) * rows
                out[:, start : start + small] = own[row : row + rows, :].astype(out.dtype)

    arrive(zout.at[:, pl.ds(0, groups - 1)], os_)


def shards(tokens, routes, gate_scores, w_gate, w_up, w_down):
    rows, width = tokens.shape
    top = routes.shape[1]
    hidden = w_gate.shape[2]
    owners, groups = lax.axis_size("expert"), lax.axis_size("dp")
    cap = rows // 4 + 1
    sizes = (groups, owners, rows, top, width, hidden, cap)
    per, fold, tall, wide, halves, small, chunk, parts = layout(sizes)
    total, columns = owners * tall, groups * 16
    vmem = lambda shape, dtype=BF16: pltpu.VMEM(shape, dtype)
    dma = pltpu.SemaphoreType.DMA
    flops = 6 * owners * per * width * hidden
    return pl.pallas_call(
        functools.partial(kernel, sizes),
        out_shape=jax.ShapeDtypeStruct((rows, width), BF16),
        in_specs=[
            pl.BlockSpec(memory_space=pltpu.VMEM),
            pl.BlockSpec(memory_space=pltpu.SMEM),
            pl.BlockSpec(memory_space=pltpu.SMEM),
        ] + [pl.BlockSpec(memory_space=pl.ANY)] * 3,
        out_specs=pl.BlockSpec(memory_space=pltpu.VMEM),
        scratch_shapes=[
            vmem((width, hidden)), vmem((width, hidden)), vmem((hidden, width)),
            vmem((parts, groups, 16, small)), vmem((groups, 2 * rows * top, 128), F32),
            vmem((parts, owners, tall, chunk)), vmem((parts, owners, tall, chunk)),
            vmem((parts, owners, tall, chunk)), vmem((parts, owners, tall, chunk)),
            vmem((halves, total, columns)), vmem((halves, 2 * columns, total)),
            vmem((owners * per, hidden), F32), vmem((owners * per, hidden), F32),
            vmem((owners * per, hidden)), vmem((parts, columns, small), F32),
            vmem((parts, groups, 16, small)), vmem((parts, groups, 16, small)),
            dma((3,)), dma, dma((parts,)), dma, dma,
            dma, dma((parts,)), dma, dma((parts,)), dma, dma((parts,)),
        ],
        compiler_params=pltpu.CompilerParams(
            collective_id=0, has_side_effects=True, vmem_limit_bytes=60 * 2**20),
        cost_estimate=pl.CostEstimate(
            flops=flops, bytes_accessed=6 * width * hidden, transcendentals=owners * per * hidden),
    )(tokens, routes.T, gate_scores.T, w_gate, w_up, w_down)


def solution(mesh):
    return jax.shard_map(
        shards,
        mesh=mesh,
        in_specs=(
            P(("dp", "expert"), None),
            P(("dp", "expert"), None),
            P(("dp", "expert"), None),
            P("expert", None, "dp"),
            P("expert", None, "dp"),
            P("expert", "dp", None),
        ),
        out_specs=P(("dp", "expert"), None),
        check_vma=False,
    )
```
